256 devices in a mesh: dp: 64 (over z, x, core), tensor: 4 (over y).
Axes of the slice: x: 4, y: 4, z: 8, core: 2. Of those that a mesh axis runs over, the one named last changes fastest.
Arguments:
- tokens: bfloat16 [65536, 896], P('dp'), may hold values from -6 to 6
- hidden_grad: bfloat16 [65536, 2432], P('dp', 'tensor'), may hold values from -6 to 6
- gate_weight: bfloat16 [896, 2432], P(None, 'tensor'), may hold values from -0.1875 to 0.1875
- up_weight: bfloat16 [896, 2432], P(None, 'tensor'), may hold values from -0.1875 to 0.1875
- gate_error: bfloat16 [64, 896, 2432], P('dp', None, 'tensor'), may hold values from -2 to 2
- up_error: bfloat16 [64, 896, 2432], P('dp', None, 'tensor'), may hold values from -2 to 2
- gate_basis: float32 [32, 2432], P(None, 'tensor'), may hold values from -6 to 6
- up_basis: float32 [32, 2432], P(None, 'tensor'), may hold values from -6 to 6
Outputs:
- input_grad: bfloat16 [65536, 896], P(('dp', 'tensor'))
- gate_update: bfloat16 [896, 2432], P(None, 'tensor')
- up_update: bfloat16 [896, 2432], P(None, 'tensor')
- gate_error_next: bfloat16 [64, 896, 2432], P('dp', None, 'tensor')
- up_error_next: bfloat16 [64, 896, 2432], P('dp', None, 'tensor')
The draws below stay inside these ranges and needn't reach their ends.
All inputs are finite; a program needn't handle non-finite values.
Results may differ from the reference program's by a relative error of at most 0.0053.
Values sent between devices are 32-bit elements; how exact they have to be, the bound alone decides.
A program may use at most 128 MiB of HBM per device.

```python
import math
import jax
import jax.numpy as jnp
from jax import lax

D = 896
FF = 2432
RANK = 32
TOK_DEV = 1024
REPLICAS = 64
TOKENS = 65536


def draw_gate_error(key, part):
    key = jax.random.fold_in(key, 11)
    private_key = jax.random.fold_in(key, 1)
    private = jnp.clip(jax.random.normal(private_key, (REPLICAS, D, FF), jnp.float32), -4.0, 4.0)
    return (0.5 * private).astype(jnp.bfloat16)


def draw_up_error(key, part):
    key = jax.random.fold_in(key, 23)
    private_key = jax.random.fold_in(key, 1)
    private = jnp.clip(jax.random.normal(private_key, (REPLICAS, D, FF), jnp.float32), -4.0, 4.0)
    return (0.5 * private).astype(jnp.bfloat16)


def block_scale(stream_key, extent, cuts, least, top_value):
    def one(dim, blocks):
        draws = jax.random.uniform(jax.random.fold_in(jax.random.fold_in(stream_key, 6), dim), (blocks,), jnp.float32, least / len(cuts), top_value / len(cuts))
        return jnp.repeat(jnp.exp(draws), extent[dim] // blocks).reshape((-1,) + (1,) * (len(extent) - dim - 1))

    level = one(*cuts[0])
    for cut in cuts[1:]:
        level = level * one(*cut)
    return level


def bell_draw(key, shape, deviation, bound, shards=(), held_as=jnp.bfloat16):
    factor_of = block_scale(key, shape, shards, -0.22, 0.18) if shards else 1.0
    drawn = jax.random.normal(key, shape, jnp.float32) * deviation * factor_of
    return jnp.minimum(jnp.maximum(drawn, -bound), bound).astype(held_as)


def setup_inputs(seed: int = 0) -> dict:
    seeds = jax.random.split(jax.random.key(seed), 9)
    return {
        "tokens": bell_draw(seeds[0], (TOKENS, D), 1.0, 6.0, ((0, 64),)),
        "hidden_grad": bell_draw(seeds[1], (TOKENS, FF), 1.0, 6.0, ((0, 64), (1, 4))),
        "gate_weight": bell_draw(seeds[2], (D, FF), D ** -0.5, 0.1875, ((1, 4),)),
        "up_weight": bell_draw(seeds[3], (D, FF), D ** -0.5, 0.1875, ((1, 4),)),
        "gate_error": draw_gate_error(jax.random.fold_in(seeds[8], 71), 0),
        "up_error": draw_up_error(jax.random.fold_in(seeds[8], 71), 0),
        "gate_basis": bell_draw(seeds[6], (RANK, FF), 1.0, 6.0, ((1, 4),), jnp.float32),
        "up_basis": bell_draw(seeds[7], (RANK, FF), 1.0, 6.0, ((1, 4),), jnp.float32),
    }


def compress(tokens, deltas, error, basis):
    grad_scale = 1.0 / math.sqrt(TOK_DEV)
    local_tokens = tokens.reshape(REPLICAS, TOK_DEV, D)
    local_deltas = deltas.reshape(REPLICAS, TOK_DEV, FF)

    def replica_grad(bundle):
        tok_rows, delta_rows, error_rows = bundle
        product = jnp.dot(tok_rows.T.astype(jnp.float32), delta_rows.astype(jnp.float32), preferred_element_type=jnp.float32)
        return product * grad_scale + error_rows.astype(jnp.float32)
    replica_grads = lax.map(replica_grad, (local_tokens, local_deltas, error))
    summed_grad = lax.optimization_barrier(jnp.sum(replica_grads, axis=0))
    factor = jnp.dot(basis.astype(jnp.float32), summed_grad.T.astype(jnp.float32), precision=lax.Precision.HIGHEST, preferred_element_type=jnp.float32)
    gram_matrix = jnp.dot(factor.astype(jnp.float32), factor.T.astype(jnp.float32), precision=lax.Precision.HIGHEST, preferred_element_type=jnp.float32)
    triangle = jnp.linalg.cholesky(gram_matrix)
    factor_hat = jax.scipy.linalg.solve_triangular(triangle, factor, lower=True)
    coef = jnp.dot(factor_hat.astype(jnp.float32), summed_grad.astype(jnp.float32), precision=lax.Precision.HIGHEST, preferred_element_type=jnp.float32)
    approx = jnp.dot(factor_hat.T.astype(jnp.float32), coef.astype(jnp.float32), precision=lax.Precision.HIGHEST, preferred_element_type=jnp.float32)
    error_next = (replica_grads - approx[None] / REPLICAS).astype(jnp.bfloat16)
    return (approx.astype(jnp.bfloat16), error_next)

def reference(tokens, hidden_grad, gate_weight, up_weight, gate_error, up_error, gate_basis, up_basis):
    gate_act = jnp.dot(tokens.astype(jnp.float32), gate_weight.astype(jnp.float32), preferred_element_type=jnp.float32)
    up_act = jnp.dot(tokens.astype(jnp.float32), up_weight.astype(jnp.float32), preferred_element_type=jnp.float32)
    squash = jax.nn.sigmoid(gate_act)
    cotangent = hidden_grad.astype(jnp.float32)
    gate_delta = (cotangent * up_act * squash * (1.0 + gate_act * (1.0 - squash))).astype(jnp.bfloat16)
    up_delta = (cotangent * gate_act * squash).astype(jnp.bfloat16)
    input_grad = (jnp.dot(gate_delta.astype(jnp.float32), gate_weight.T.astype(jnp.float32), preferred_element_type=jnp.float32) + jnp.dot(up_delta.astype(jnp.float32), up_weight.T.astype(jnp.float32), preferred_element_type=jnp.float32)).astype(jnp.bfloat16)
    gate_update, gate_error_next = compress(tokens, gate_delta, gate_error, gate_basis)
    up_update, up_error_next = compress(tokens, up_delta, up_error, up_basis)
    return (input_grad, gate_update, up_update, gate_error_next, up_error_next)
```

```python
import functools
import math

import jax
import jax.numpy as jnp
from jax import lax
from jax.experimental import pallas as pl
from jax.experimental.pallas import tpu as pltpu
from jax.sharding import PartitionSpec as P

MESH = pl.DeviceIdType.MESH
F32 = jnp.float32
BF16 = jnp.bfloat16
HIGH = lax.Precision.HIGHEST
NZ, NX, NC, NY = 8, 4, 2, 4
D, FF, RANK, TOK = 896, 608, 32, 1024
ROWS = TOK // NY
HALF = ROWS // 2
SHARE = RANK // (NX * NY)
CROWS = RANK // NX
SCALE = 1.0 / math.sqrt(TOK)


def mm(a, b, ca, cb, precision=None):
    return lax.dot_general(
        a, b, (((ca,), (cb,)), ((), ())), precision=precision, preferred_element_type=F32
    )


def split_rows(a):
    high = a.astype(BF16)
    low = (a - high.astype(F32)).astype(BF16)
    return jnp.concatenate([high, low], axis=0)


def fold(a):
    return a[:RANK] + a[RANK:]


def device(z, x, c, y):
    return ((z * NX + x) * NC + c, y)


def main_kernel(
    tok_h, hid_h, wg_h, wu_h, eg_h, eu_h, bg_h, bu_h,
    ig_o, full_o, coef_o, stack_o,
    tok, hid, wgt, err, basis, delta, part, half_in, whole_in, ig_b,
    full, mate_full, s_high, s_low,
    f_out, f_in, f_src, f_rs, f_z, f_ag, fac, elim, h_own, h_all, stack,
    c_src, c_rs, c_z, c_all,
    in_sem, out_sem, send_sem, recv_sem,
):
    dp = lax.axis_index("dp")
    y = lax.axis_index("tensor")
    c = lax.rem(dp, NC)
    x = lax.rem(lax.div(dp, NC), NX)
    z = lax.div(dp, NC * NX)
    mate = 1 - c

    loads = [
        pltpu.make_async_copy(src, dst, in_sem.at[i])
        for i, (src, dst) in enumerate(
            [
                (wg_h, wgt.at[pl.ds(0, FF)]),
                (wu_h, wgt.at[pl.ds(FF, FF)]),
                (tok_h, tok),
                (hid_h, hid),
                (bg_h, basis.at[0]),
                (bu_h, basis.at[1]),
                (eg_h.at[0], err.at[0]),
                (eu_h.at[0], err.at[1]),
            ]
        )
    ]
    for load in loads:
        load.start()

    def at_xy(dx, dy):
        return device(z, lax.rem(x + dx, NX), c, lax.rem(y + dy, NY))

    def at_z(dz):
        return device(lax.rem(z + dz, NZ), x, c, y)

    def at_cx(dc, dx):
        return device(z, lax.rem(x + dx, NX), lax.rem(c + dc, NC), y)

    xy = [(dx, dy) for dx in range(NX) for dy in range(NY)][1:]
    cx = [(dc, dx) for dc in range(NC) for dx in range(NX)][1:]
    greet = [at_xy(*o) for o in xy] + [at_z(dz) for dz in range(1, NZ)]
    greet += [at_cx(*o) for o in cx if o[0] == 1]
    barrier = pltpu.get_barrier_semaphore()
    for other in greet:
        pl.semaphore_signal(barrier, inc=1, device_id=other, device_id_type=MESH)

    used = [0]
    sent = []

    def send(src, dst, to):
        i = used[0]
        used[0] += 1
        copy = pltpu.make_async_remote_copy(
            src_ref=src, dst_ref=dst, send_sem=send_sem.at[i], recv_sem=recv_sem.at[i],
            device_id=to, device_id_type=MESH,
        )
        copy.start()
        sent.append(copy)
        return copy

    for load in loads[:4]:
        load.wait()

    def act_step(i, carry):
        cols = pl.ds(pl.multiple_of(i * ROWS, ROWS), ROWS)
        act = mm(wgt[...], tok[cols, :], 1, 1)
        g, u = act[:FF], act[FF:]
        h = hid[:, cols].astype(F32)
        s = 1.0 / (1.0 + jnp.exp(-g))
        hs = h * s
        delta[:FF, cols] = (hs * u * (1.0 + g * (1.0 - s))).astype(BF16)
        delta[FF:, cols] = (hs * g).astype(BF16)
        return carry

    with jax.named_scope("acts"):
        lax.fori_loop(0, NY, act_step, 0)
    for load in loads[4:]:
        load.wait()

    def pick(p):
        return pl.ds(pl.multiple_of(p * FF, FF), FF)

    def factor_of(p):
        b = split_rows(basis[p])
        t = fold(mm(b, delta[pick(p), :], 1, 0))
        e = fold(mm(b, err[p], 1, 0))
        return fold(mm(split_rows(t), tok[...], 1, 0)) * SCALE + e

    f_out[...] = factor_of(mate)
    pl.semaphore_wait(barrier, len(greet))
    ex_f = send(f_out, f_in, at_cx(1, 0))
    own = factor_of(c)
    ex_f.wait_recv()
    own = own + f_in[...]
    for s in range(NX * NY):
        f_src[s] = own[s * SHARE:(s + 1) * SHARE]
    rs = []
    for i, (dx, dy) in enumerate(xy):
        to = lax.rem(x + dx, NX) * NY + lax.rem(y + dy, NY)
        rs.append(send(f_src.at[to], f_rs.at[i], at_xy(dx, dy)))

    def partial(k):
        cols = pl.ds(pl.multiple_of(lax.rem(y + k, NY) * ROWS, ROWS), ROWS)
        part[k] = mm(delta[:, cols], wgt[...], 0, 0)

    low, high = pl.ds(0, HALF), pl.ds(HALF, HALF)
    partial(2)
    far_up = send(part.at[2, low], half_in.at[0], at_xy(0, 1))
    far_down = send(part.at[2, high], half_in.at[1], at_xy(0, NY - 1))
    partial(1)
    partial(3)

    mine = x * NY + y
    total = f_src[mine]
    for copy in rs:
        copy.wait_recv()
    for i in range(len(xy)):
        total = total + f_rs[i]
    f_z[z] = total
    zs = [send(f_z.at[z], f_z.at[z], at_z(dz)) for dz in range(1, NZ)]

    def grad_of(p):
        full[p] = mm(delta[pick(p), :], tok[...], 1, 0) * SCALE + err[p].astype(F32)

    grad_of(mate)
    ex_s = send(full.at[mate], mate_full, at_cx(1, 0))
    grad_of(c)

    for copy in zs:
        copy.wait_recv()
    total = f_z[0]
    for i in range(1, NZ):
        total = total + f_z[i]
    f_ag[mine] = total
    ag = [send(f_ag.at[mine], f_ag.at[mine], at_xy(dx, dy)) for dx, dy in xy]

    near_up = [send(part.at[1, high], whole_in.at[0, high], at_xy(0, 1))]
    near_down = [send(part.at[3, low], whole_in.at[1, low], at_xy(0, NY - 1))]
    far_up.wait_recv()
    part[1, low] = part[1, low] + half_in[0]
    near_up.append(send(part.at[1, low], whole_in.at[0, low], at_xy(0, 1)))
    far_down.wait_recv()
    part[3, high] = part[3, high] + half_in[1]
    near_down.append(send(part.at[3, high], whole_in.at[1, high], at_xy(0, NY - 1)))

    stores = [
        pltpu.make_async_copy(full, full_o, out_sem.at[0]),
        pltpu.make_async_copy(ig_b, ig_o, out_sem.at[1]),
        pltpu.make_async_copy(c_all, coef_o, out_sem.at[2]),
        pltpu.make_async_copy(stack, stack_o, out_sem.at[3]),
    ]
    stores[0].start()
    ex_s.wait_recv()
    both = (full[c] + mate_full[...]).T
    top = both.astype(BF16)
    s_high[...] = top
    s_low[...] = (both - top.astype(F32)).astype(BF16)
    partial(0)

    for copy in ag:
        copy.wait_recv()
    for s in range(NX * NY):
        fac[s * SHARE:(s + 1) * SHARE] = f_ag[s]
    factor = fac[...]
    pair = split_rows(factor)
    coef = fold(mm(pair, s_high[...], 1, 0)) + mm(pair[:RANK], s_low[...], 1, 0)
    for j in range(NX):
        c_src[j] = coef[j * CROWS:(j + 1) * CROWS]
    crs = [
        send(c_src.at[lax.rem(x + dx, NX)], c_rs.at[x], at_cx(0, dx)) for dx in range(1, NX)
    ]
    c_rs[x] = c_src[x]

    sub = lax.broadcasted_iota(jnp.int32, (RANK, 2 * RANK), 0)
    lane = lax.broadcasted_iota(jnp.int32, (RANK, 2 * RANK), 1)
    gram = mm(factor, factor, 1, 1, HIGH)
    elim[:, :RANK] = gram
    elim[:, RANK:] = (sub[:, :RANK] == lane[:, :RANK]).astype(F32)

    def eliminate(k, a):
        row = jnp.sum(jnp.where(sub == k, a, 0.0), axis=0, keepdims=True)
        column = jnp.sum(jnp.where(lane == k, a, 0.0), axis=1, keepdims=True)
        pivot = jnp.sum(jnp.where(lane[:1] == k, row, 0.0), axis=1, keepdims=True)
        return a - jnp.where(sub > k, (column / pivot) * row, 0.0)

    state = lax.fori_loop(0, RANK // 2, eliminate, elim[...])
    for copy in crs:
        copy.wait_recv()
    total = c_rs[0]
    for i in range(1, NX):
        total = total + c_rs[i]
    c_z[z] = total
    czs = [send(c_z.at[z], c_z.at[z], at_z(dz)) for dz in range(1, NZ)]

    state = lax.fori_loop(RANK // 2, RANK, eliminate, state)
    left, inverse = state[:, :RANK], state[:, RANK:]
    pivots = jnp.sum(
        jnp.where(sub[:, :RANK] == lane[:, :RANK], left, 0.0), axis=1, keepdims=True
    )
    inverse = inverse * lax.rsqrt(pivots)
    hat = mm(inverse, factor, 1, 0, HIGH)
    h_own[...] = mm(inverse, hat, 0, 0, HIGH)
    ex_h = send(h_own, h_all, at_cx(1, 0))

    for copy in czs:
        copy.wait_recv()
    total = c_z[0]
    for i in range(1, NZ):
        total = total + c_z[i]
    c_all[c, x] = total
    cag = [send(c_all.at[c, x], c_all.at[c, x], at_cx(dc, dx)) for dc, dx in cx]

    ex_h.wait_recv()
    for p, value in ((c, h_own[...]), (mate, h_all[...])):
        top = value.astype(BF16)
        stack[p, :RANK] = top
        stack[p, RANK:2 * RANK] = top
        stack[p, 2 * RANK:] = (value - top.astype(F32)).astype(BF16)
    stores[3].start()

    for copy in near_up + near_down:
        copy.wait_recv()
    ig_b[...] = (part[0] + (whole_in[0] + whole_in[1])).astype(BF16)
    stores[1].start()
    for copy in cag:
        copy.wait_recv()
    stores[2].start()
    for copy in sent:
        copy.wait_send()
    for store in stores:
        store.wait()


def final_kernel(ig, full, coef, stack, ig_o, gu_o, uu_o, ge_o, ue_o):
    @pl.when(pl.program_id(0) == 0)
    def _():
        ig_o[...] = ig[...]

    for p, (update, error) in enumerate(((gu_o, ge_o), (uu_o, ue_o))):
        value = coef[p]
        top = value.astype(BF16)
        low = (value - top.astype(F32)).astype(BF16)
        approx = mm(jnp.concatenate([top, low, top], axis=0), stack[p], 0, 0)
        update[...] = approx.astype(BF16)
        error[0] = (full[p] - approx * (1.0 / (NZ * NX * NC))).astype(BF16)


def on_device(tokens, hidden_grad, gate_weight, up_weight, gate_error, up_error, gate_basis, up_basis):
    V, S = pltpu.VMEM, pltpu.SemaphoreType.DMA
    any_spec = pl.BlockSpec(memory_space=pl.ANY)
    copies = 80
    ig, full, coef, stack = pl.pallas_call(
        main_kernel,
        name="main",
        out_shape=(
            jax.ShapeDtypeStruct((ROWS, D), BF16),
            jax.ShapeDtypeStruct((2, FF, D), F32),
            jax.ShapeDtypeStruct((2, NX, CROWS, FF), F32),
            jax.ShapeDtypeStruct((2, 3 * RANK, D), BF16),
        ),
        in_specs=[any_spec] * 8,
        out_specs=(any_spec,) * 4,
        scratch_shapes=[
            V((TOK, D), BF16), V((FF, TOK), BF16), V((2 * FF, D), BF16),
            V((2, FF, D), BF16), V((2, RANK, FF), F32), V((2 * FF, TOK), BF16),
            V((NY, ROWS, D), F32), V((2, HALF, D), F32), V((2, ROWS, D), F32), V((ROWS, D), BF16),
            V((2, FF, D), F32), V((FF, D), F32), V((D, FF), BF16), V((D, FF), BF16),
            V((RANK, D), F32), V((RANK, D), F32), V((NX * NY, SHARE, D), F32),
            V((NX * NY - 1, SHARE, D), F32), V((NZ, SHARE, D), F32), V((NX * NY, SHARE, D), F32),
            V((RANK, D), F32), V((RANK, 2 * RANK), F32), V((RANK, D), F32), V((RANK, D), F32),
            V((2, 3 * RANK, D), BF16),
            V((NX, CROWS, FF), F32), V((NX, CROWS, FF), F32), V((NZ, CROWS, FF), F32),
            V((2, NX, CROWS, FF), F32),
            S((8,)), S((4,)), S((copies,)), S((copies,)),
        ],
        compiler_params=pltpu.CompilerParams(
            collective_id=0, has_side_effects=True, vmem_limit_bytes=56 << 20
        ),
        cost_estimate=pl.CostEstimate(
            flops=8 * TOK * D * FF, bytes_accessed=16 << 20, transcendentals=TOK * FF
        ),
    )(
        tokens, hidden_grad.T, gate_weight.T, up_weight.T,
        jnp.swapaxes(gate_error, 1, 2), jnp.swapaxes(up_error, 1, 2), gate_basis, up_basis,
    )
    block = 128
    out = jax.ShapeDtypeStruct((FF, D), BF16)
    out_error = jax.ShapeDtypeStruct((1, FF, D), BF16)
    rows = pl.BlockSpec((block, D), lambda i: (i, 0))
    rows_error = pl.BlockSpec((1, block, D), lambda i: (0, i, 0))
    whole = pl.BlockSpec((ROWS, D), lambda i: (0, 0))
    input_grad, gate_update, up_update, gate_next, up_next = pl.pallas_call(
        final_kernel,
        name="outputs",
        grid=(pl.cdiv(FF, block),),
        out_shape=(jax.ShapeDtypeStruct((ROWS, D), BF16), out, out, out_error, out_error),
        in_specs=[
            whole,
            pl.BlockSpec((2, block, D), lambda i: (0, i, 0)),
            pl.BlockSpec((2, RANK, block), lambda i: (0, 0, i)),
            pl.BlockSpec((2, 3 * RANK, D), lambda i: (0, 0, 0)),
        ],
        out_specs=(whole, rows, rows, rows_error, rows_error),
        compiler_params=pltpu.CompilerParams(vmem_limit_bytes=56 << 20),
    )(ig, full, coef.reshape(2, RANK, FF), stack)
    return (
        input_grad, gate_update.T, up_update.T,
        jnp.swapaxes(gate_next, 1, 2), jnp.swapaxes(up_next, 1, 2),
    )


def solution(mesh):
    placed = (
        P("dp", None),
        P("dp", "tensor"),
        P(None, "tensor"),
        P(None, "tensor"),
        P("dp", None, "tensor"),
        P("dp", None, "tensor"),
        P(None, "tensor"),
        P(None, "tensor"),
    )
    return jax.shard_map(
        on_device,
        mesh=mesh,
        in_specs=placed,
        out_specs=(
            P(("dp", "tensor"), None),
            P(None, "tensor"),
            P(None, "tensor"),
            P("dp", None, "tensor"),
            P("dp", None, "tensor"),
        ),
        check_vma=False,
    )
```

```python
import functools
import math

import jax
import jax.numpy as jnp
from jax import lax
from jax.experimental import pallas as pl
from jax.experimental.pallas import tpu as pltpu
from jax.sharding import PartitionSpec as P

MESH = pl.DeviceIdType.MESH
F32 = jnp.float32
BF16 = jnp.bfloat16
HIGH = lax.Precision.HIGHEST
NZ, NX, NC, NY = 8, 4, 2, 4
D, FF, RANK, TOK = 896, 608, 32, 1024
ROWS = TOK // NY
HALF = ROWS // 2
SHARE = RANK // (NX * NY)
CROWS = RANK // NX
SCALE = 1.0 / math.sqrt(TOK)
BLOCKS = ((0, 160), (160, 160), (320, 160), (480, 128))


def mm(a, b, ca, cb, precision=None):
    return lax.dot_general(
        a, b, (((ca,), (cb,)), ((), ())), precision=precision, preferred_element_type=F32
    )


def split_rows(a):
    high = a.astype(BF16)
    low = (a - high.astype(F32)).astype(BF16)
    return jnp.concatenate([high, low], axis=0)


def fold(a):
    return a[:RANK] + a[RANK:]


def device(z, x, c, y):
    return ((z * NX + x) * NC + c, y)


def main_kernel(
    tok_h, hid_h, wg_h, wu_h, eg_h, eu_h, bg_h, bu_h,
    ig_o, full_o, coef_o, stack_o,
    tok, hid, wgt, err, basis, delta, part, half_in, whole_in, ig_b,
    full, mate_full, s_high, s_low,
    f_out, f_in, f_src, f_rs, f_z, f_ag, fac, elim, h_own, h_all, stack,
    c_src, c_rs, c_z, c_all,
    in_sem, out_sem, send_sem, recv_sem,
):
    dp = lax.axis_index("dp")
    y = lax.axis_index("tensor")
    c = lax.rem(dp, NC)
    x = lax.rem(lax.div(dp, NC), NX)
    z = lax.div(dp, NC * NX)
    mate = 1 - c

    loads = [
        pltpu.make_async_copy(src, dst, in_sem.at[i])
        for i, (src, dst) in enumerate(
            [
                (wg_h, wgt.at[pl.ds(0, FF)]),
                (wu_h, wgt.at[pl.ds(FF, FF)]),
                (tok_h, tok),
                (hid_h, hid),
                (bg_h, basis.at[0]),
                (bu_h, basis.at[1]),
                (eg_h.at[0], err.at[0]),
                (eu_h.at[0], err.at[1]),
            ]
        )
    ]
    for load in loads:
        load.start()

    def at_xy(dx, dy):
        return device(z, lax.rem(x + dx, NX), c, lax.rem(y + dy, NY))

    def at_z(dz):
        return device(lax.rem(z + dz, NZ), x, c, y)

    def at_cx(dc, dx):
        return device(z, lax.rem(x + dx, NX), lax.rem(c + dc, NC), y)

    xy = [(dx, dy) for dx in range(NX) for dy in range(NY)][1:]
    cx = [(dc, dx) for dc in range(NC) for dx in range(NX)][1:]
    greet = [at_xy(*o) for o in xy] + [at_z(dz) for dz in range(1, NZ)]
    greet += [at_cx(*o) for o in cx if o[0] == 1]
    barrier = pltpu.get_barrier_semaphore()
    for other in greet:
        pl.semaphore_signal(barrier, inc=1, device_id=other, device_id_type=MESH)

    used = [0]
    sent = []

    def send(src, dst, to):
        i = used[0]
        used[0] += 1
        copy = pltpu.make_async_remote_copy(
            src_ref=src, dst_ref=dst, send_sem=send_sem.at[i], recv_sem=recv_sem.at[i],
            device_id=to, device_id_type=MESH,
        )
        copy.start()
        sent.append(copy)
        return copy

    for load in loads[:4]:
        load.wait()

    def act_step(i, carry):
        cols = pl.ds(pl.multiple_of(i * ROWS, ROWS), ROWS)
        act = mm(wgt[...], tok[cols, :], 1, 1)
        g, u = act[:FF], act[FF:]
        h = hid[:, cols].astype(F32)
        s = 1.0 / (1.0 + jnp.exp(-g))
        hs = h * s
        delta[:FF, cols] = (hs * u * (1.0 + g * (1.0 - s))).astype(BF16)
        delta[FF:, cols] = (hs * g).astype(BF16)
        return carry

    with jax.named_scope("acts"):
        lax.fori_loop(0, NY, act_step, 0)
    for load in loads[4:]:
        load.wait()

    def pick(p):
        return pl.ds(pl.multiple_of(p * FF, FF), FF)

    def factor_of(p):
        b = split_rows(basis[p])
        t = fold(mm(b, delta[pick(p), :], 1, 0))
        e = fold(mm(b, err[p], 1, 0))
        return fold(mm(split_rows(t), tok[...], 1, 0)) * SCALE + e

    f_out[...] = factor_of(mate)
    pl.semaphore_wait(barrier, len(greet))
    ex_f = send(f_out, f_in, at_cx(1, 0))
    own = factor_of(c)
    ex_f.wait_recv()
    own = own + f_in[...]
    for s in range(NX * NY):
        f_src[s] = own[s * SHARE:(s + 1) * SHARE]
    rs = []
    for i, (dx, dy) in enumerate(xy):
        to = lax.rem(x + dx, NX) * NY + lax.rem(y + dy, NY)
        rs.append(send(f_src.at[to], f_rs.at[i], at_xy(dx, dy)))

    def partial(k):
        cols = pl.ds(pl.multiple_of(lax.rem(y + k, NY) * ROWS, ROWS), ROWS)
        part[k] = mm(delta[:, cols], wgt[...], 0, 0)

    low, high = pl.ds(0, HALF), pl.ds(HALF, HALF)
    partial(2)
    far_up = send(part.at[2, low], half_in.at[0], at_xy(0, 1))
    far_down = send(part.at[2, high], half_in.at[1], at_xy(0, NY - 1))
    partial(1)
    partial(3)

    mine = x * NY + y
    total = f_src[mine]
    for copy in rs:
        copy.wait_recv()
    for i in range(len(xy)):
        total = total + f_rs[i]
    f_z[z] = total
    zs = [send(f_z.at[z], f_z.at[z], at_z(dz)) for dz in range(1, NZ)]

    def grad_of(p):
        full[p] = mm(delta[pick(p), :], tok[...], 1, 0) * SCALE + err[p].astype(F32)

    grad_of(mate)
    ex_s = send(full.at[mate], mate_full, at_cx(1, 0))
    grad_of(c)

    for copy in zs:
        copy.wait_recv()
    total = f_z[0]
    for i in range(1, NZ):
        total = total + f_z[i]
    f_ag[mine] = total
    ag = [send(f_ag.at[mine], f_ag.at[mine], at_xy(dx, dy)) for dx, dy in xy]

    near_up = [send(part.at[1, high], whole_in.at[0, high], at_xy(0, 1))]
    near_down = [send(part.at[3, low], whole_in.at[1, low], at_xy(0, NY - 1))]
    far_up.wait_recv()
    part[1, low] = part[1, low] + half_in[0]
    near_up.append(send(part.at[1, low], whole_in.at[0, low], at_xy(0, 1)))
    far_down.wait_recv()
    part[3, high] = part[3, high] + half_in[1]
    near_down.append(send(part.at[3, high], whole_in.at[1, high], at_xy(0, NY - 1)))

    stores = [
        pltpu.make_async_copy(full, full_o, out_sem.at[0]),
        pltpu.make_async_copy(ig_b, ig_o, out_sem.at[1]),
        pltpu.make_async_copy(c_all, coef_o, out_sem.at[2]),
        pltpu.make_async_copy(stack, stack_o, out_sem.at[3]),
    ]
    stores[0].start()
    ex_s.wait_recv()
    both = (full[c] + mate_full[...]).T
    top = both.astype(BF16)
    s_high[...] = top
    s_low[...] = (both - top.astype(F32)).astype(BF16)
    partial(0)

    for copy in ag:
        copy.wait_recv()
    for s in range(NX * NY):
        fac[s * SHARE:(s + 1) * SHARE] = f_ag[s]
    factor = fac[...]
    pair = split_rows(factor)
    coef = fold(mm(pair, s_high[...], 1, 0)) + mm(pair[:RANK], s_low[...], 1, 0)
    for j in range(NX):
        c_src[j] = coef[j * CROWS:(j + 1) * CROWS]
    crs = [
        send(c_src.at[lax.rem(x + dx, NX)], c_rs.at[x], at_cx(0, dx)) for dx in range(1, NX)
    ]
    c_rs[x] = c_src[x]

    sub = lax.broadcasted_iota(jnp.int32, (RANK, 2 * RANK), 0)
    lane = lax.broadcasted_iota(jnp.int32, (RANK, 2 * RANK), 1)
    gram = mm(factor, factor, 1, 1, HIGH)
    elim[:, :RANK] = gram
    elim[:, RANK:] = (sub[:, :RANK] == lane[:, :RANK]).astype(F32)

    def eliminate(k, a):
        row = jnp.sum(jnp.where(sub == k, a, 0.0), axis=0, keepdims=True)
        column = jnp.sum(jnp.where(lane == k, a, 0.0), axis=1, keepdims=True)
        pivot = jnp.sum(jnp.where(lane[:1] == k, row, 0.0), axis=1, keepdims=True)
        return a - jnp.where(sub > k, (column / pivot) * row, 0.0)

    state = lax.fori_loop(0, RANK // 2, eliminate, elim[...])
    for copy in crs:
        copy.wait_recv()
    total = c_rs[0]
    for i in range(1, NX):
        total = total + c_rs[i]
    c_z[z] = total
    czs = [send(c_z.at[z], c_z.at[z], at_z(dz)) for dz in range(1, NZ)]

    state = lax.fori_loop(RANK // 2, RANK, eliminate, state)
    left, inverse = state[:, :RANK], state[:, RANK:]
    pivots = jnp.sum(
        jnp.where(sub[:, :RANK] == lane[:, :RANK], left, 0.0), axis=1, keepdims=True
    )
    inverse = inverse * lax.rsqrt(pivots)
    hat = mm(inverse, factor, 1, 0, HIGH)
    h_own[...] = mm(inverse, hat, 0, 0, HIGH)
    ex_h = send(h_own, h_all, at_cx(1, 0))

    for copy in czs:
        copy.wait_recv()
    total = c_z[0]
    for i in range(1, NZ):
        total = total + c_z[i]
    c_all[c, x] = total
    cag = [send(c_all.at[c, x], c_all.at[c, x], at_cx(dc, dx)) for dc, dx in cx]

    ex_h.wait_recv()
    for p, value in ((c, h_own[...]), (mate, h_all[...])):
        top = value.astype(BF16)
        stack[p, :RANK] = top
        stack[p, RANK:2 * RANK] = top
        stack[p, 2 * RANK:] = (value - top.astype(F32)).astype(BF16)
    stores[3].start()

    for copy in near_up + near_down:
        copy.wait_recv()
    ig_b[...] = (part[0] + (whole_in[0] + whole_in[1])).astype(BF16)
    stores[1].start()
    for copy in cag:
        copy.wait_recv()
    stores[2].start()
    for copy in sent:
        copy.wait_send()
    for store in stores:
        store.wait()


def final_kernel(
    ig, full, coef, stack, ig_o, gu_o, uu_o, ge_o, ue_o, left, update_v, error_v, out_sem
):
    stores = [pltpu.make_async_copy(ig, ig_o, out_sem.at[4 * len(BLOCKS)])]
    stores[0].start()
    for p in range(2):
        value = coef[p]
        top = value.astype(BF16)
        low = (value - top.astype(F32)).astype(BF16)
        left[p] = jnp.concatenate([top, low, top], axis=0).T
    k = 0
    for start, size in BLOCKS:
        for p, (update, error) in enumerate(((gu_o, ge_o), (uu_o, ue_o))):
            rows = pl.ds(start, size)
            approx = mm(left[p, rows], stack[p], 1, 0)
            update_v[p, rows] = approx.astype(BF16)
            error_v[p, rows] = (full[p, rows] - approx * (1.0 / (NZ * NX * NC))).astype(BF16)
            for src, dst in ((update_v, update), (error_v, error.at[0])):
                stores.append(pltpu.make_async_copy(src.at[p, rows], dst.at[rows], out_sem.at[k]))
                stores[-1].start()
                k += 1
    for store in stores:
        store.wait()


def on_device(tokens, hidden_grad, gate_weight, up_weight, gate_error, up_error, gate_basis, up_basis):
    V, S = pltpu.VMEM, pltpu.SemaphoreType.DMA
    any_spec = pl.BlockSpec(memory_space=pl.ANY)
    copies = 80
    ig, full, coef, stack = pl.pallas_call(
        main_kernel,
        name="main",
        out_shape=(
            V((ROWS, D), BF16), V((2, FF, D), F32), V((2, NX, CROWS, FF), F32), V((2, 3 * RANK, D), BF16),
        ),
        in_specs=[any_spec] * 8,
        out_specs=(any_spec,) * 4,
        scratch_shapes=[
            V((TOK, D), BF16), V((FF, TOK), BF16), V((2 * FF, D), BF16),
            V((2, FF, D), BF16), V((2, RANK, FF), F32), V((2 * FF, TOK), BF16),
            V((NY, ROWS, D), F32), V((2, HALF, D), F32), V((2, ROWS, D), F32), V((ROWS, D), BF16),
            V((2, FF, D), F32), V((FF, D), F32), V((D, FF), BF16), V((D, FF), BF16),
            V((RANK, D), F32), V((RANK, D), F32), V((NX * NY, SHARE, D), F32),
            V((NX * NY - 1, SHARE, D), F32), V((NZ, SHARE, D), F32), V((NX * NY, SHARE, D), F32),
            V((RANK, D), F32), V((RANK, 2 * RANK), F32), V((RANK, D), F32), V((RANK, D), F32),
            V((2, 3 * RANK, D), BF16),
            V((NX, CROWS, FF), F32), V((NX, CROWS, FF), F32), V((NZ, CROWS, FF), F32),
            V((2, NX, CROWS, FF), F32),
            S((8,)), S((4,)), S((copies,)), S((copies,)),
        ],
        compiler_params=pltpu.CompilerParams(
            collective_id=0, has_side_effects=True, vmem_limit_bytes=40 << 20
        ),
        cost_estimate=pl.CostEstimate(
            flops=8 * TOK * D * FF, bytes_accessed=16 << 20, transcendentals=TOK * FF
        ),
    )(
        *(
            pltpu.with_memory_space_constraint(a, pltpu.HBM)
            for a in (
                tokens, hidden_grad.T, gate_weight.T, up_weight.T,
                jnp.swapaxes(gate_error, 1, 2), jnp.swapaxes(up_error, 1, 2), gate_basis, up_basis,
            )
        )
    )
    out = pltpu.HBM((FF, D), BF16)
    out_error = pltpu.HBM((1, FF, D), BF16)
    input_grad, gate_update, up_update, gate_next, up_next = pl.pallas_call(
        final_kernel,
        name="outputs",
        out_shape=(pltpu.HBM((ROWS, D), BF16), out, out, out_error, out_error),
        in_specs=[pl.BlockSpec(memory_space=V)] * 4,
        out_specs=(any_spec,) * 5,
        scratch_shapes=[
            V((2, FF, 3 * RANK), BF16), V((2, FF, D), BF16), V((2, FF, D), BF16),
            S((4 * len(BLOCKS) + 1,)),
        ],
        compiler_params=pltpu.CompilerParams(vmem_limit_bytes=32 << 20),
    )(
        *(
            pltpu.with_memory_space_constraint(a, V)
            for a in (ig, full, coef.reshape(2, RANK, FF), stack)
        )
    )
    return (
        input_grad, gate_update.T, up_update.T,
        jnp.swapaxes(gate_next, 1, 2), jnp.swapaxes(up_next, 1, 2),
    )


def solution(mesh):
    placed = (
        P("dp", None),
        P("dp", "tensor"),
        P(None, "tensor"),
        P(None, "tensor"),
        P("dp", None, "tensor"),
        P("dp", None, "tensor"),
        P(None, "tensor"),
        P(None, "tensor"),
    )
    return jax.shard_map(
        on_device,
        mesh=mesh,
        in_specs=placed,
        out_specs=(
            P(("dp", "tensor"), None),
            P(None, "tensor"),
            P(None, "tensor"),
            P("dp", None, "tensor"),
            P("dp", None, "tensor"),
        ),
        check_vma=False,
    )
```

```python
import functools
import math

import jax
import jax.numpy as jnp
from jax import lax
from jax.experimental import pallas as pl
from jax.experimental.pallas import tpu as pltpu
from jax.sharding import PartitionSpec as P

MESH = pl.DeviceIdType.MESH
F32 = jnp.float32
BF16 = jnp.bfloat16
HIGH = lax.Precision.HIGHEST
NZ, NX, NC, NY = 8, 4, 2, 4
D, FF, RANK, TOK = 896, 608, 32, 1024
ROWS = TOK // NY
HALF = ROWS // 2
ORDER = (2, 1, 3, 0)
SPLIT = 10
PIECES = ((0, 32), (32, 96))
SHARE = RANK // (NX * NY)
CROWS = RANK // NX
SCALE = 1.0 / math.sqrt(TOK)
BLOCKS = ((0, 160), (160, 160), (320, 160), (480, 128))


def mm(a, b, ca, cb, precision=None):
    return lax.dot_general(
        a, b, (((ca,), (cb,)), ((), ())), precision=precision, preferred_element_type=F32
    )


def split_rows(a):
    high = a.astype(BF16)
    low = (a - high.astype(F32)).astype(BF16)
    return jnp.concatenate([high, low], axis=0)


def fold(a):
    return a[:RANK] + a[RANK:]


def device(z, x, c, y):
    return ((z * NX + x) * NC + c, y)


def main_kernel(
    tok_h, hid_h, wg_h, wu_h, eg_h, eu_h, bg_h, bu_h,
    ig_o, full_o, coef_o, stack_o,
    tok, hid, wgt, err, basis, delta, part, half_in,
    full, mate_full, s_high, s_low,
    f_out, f_in, f_src, f_rs, f_z, f_ag, fac, elim, h_own, h_all, stack,
    c_src, c_rs, c_z, c_own,
    in_sem, out_sem, send_sem, recv_sem,
):
    dp = lax.axis_index("dp")
    y = lax.axis_index("tensor")
    c = lax.rem(dp, NC)
    x = lax.rem(lax.div(dp, NC), NX)
    z = lax.div(dp, NC * NX)
    mate = 1 - c

    def chunk(k):
        return pl.ds(pl.multiple_of(lax.rem(y + k, NY) * ROWS, ROWS), ROWS)

    def local(k):
        return pl.ds(k * ROWS, ROWS)

    def load(src, dst):
        copy = pltpu.make_async_copy(src, dst, in_sem.at[len(loads)])
        copy.start()
        loads.append(copy)
        return copy

    loads = []
    load_first = [
        load(wg_h, wgt.at[pl.ds(0, FF)]), load(wu_h, wgt.at[pl.ds(FF, FF)]),
    ]
    load_chunk = {}
    for k in ORDER:
        load_chunk[k] = [
            load(tok_h.at[chunk(k)], tok.at[local(k)]),
            load(hid_h.at[:, chunk(k)], hid.at[:, local(k)]),
        ]

    def at_xy(dx, dy):
        return device(z, lax.rem(x + dx, NX), c, lax.rem(y + dy, NY))

    def at_z(dz):
        return device(lax.rem(z + dz, NZ), x, c, y)

    def at_cx(dc, dx):
        return device(z, lax.rem(x + dx, NX), lax.rem(c + dc, NC), y)

    def hops(*o):
        return -sum(min(d, n - d) for d, n in o)

    xy = [(dx, dy) for dx in range(NX) for dy in range(NY)][1:]
    xy.sort(key=lambda o: hops((o[0], NX), (o[1], NY)))
    cx = [(dc, dx) for dc in range(NC) for dx in range(NX)][1:]
    cx.sort(key=lambda o: hops((o[0], NC), (o[1], NX)))
    xs = sorted(range(1, NX), key=lambda d: hops((d, NX)))
    zs = sorted(range(1, NZ), key=lambda d: hops((d, NZ)))
    greet = [at_xy(*o) for o in xy] + [at_z(dz) for dz in range(1, NZ)]
    greet += [at_cx(*o) for o in cx if o[0] == 1]
    barrier = pltpu.get_barrier_semaphore()
    for other in greet:
        pl.semaphore_signal(barrier, inc=1, device_id=other, device_id_type=MESH)

    used = [0]
    sent = []

    def send(src, dst, to):
        i = used[0]
        used[0] += 1
        copy = pltpu.make_async_remote_copy(
            src_ref=src, dst_ref=dst, send_sem=send_sem.at[i], recv_sem=recv_sem.at[i],
            device_id=to, device_id_type=MESH,
        )
        copy.start()
        sent.append(copy)
        return copy

    def acts(k):
        cols = local(k)
        act = mm(wgt[...], tok[cols, :], 1, 1)
        g, u = act[:FF], act[FF:]
        h = hid[:, cols].astype(F32)
        s = 1.0 / (1.0 + jnp.exp(-g))
        hs = h * s
        delta[:FF, cols] = (hs * u * (1.0 + g * (1.0 - s))).astype(BF16)
        delta[FF:, cols] = (hs * g).astype(BF16)

    def partial(k):
        part[k] = mm(delta[:, local(k)], wgt[...], 0, 0)

    load_rest = [
        load(bg_h, basis.at[0]), load(bu_h, basis.at[1]),
        load(eg_h.at[0], err.at[0]), load(eu_h.at[0], err.at[1]),
    ]
    for copy in load_first:
        copy.wait()
    for k in ORDER:
        for copy in load_chunk[k]:
            copy.wait()
    acts(2)
    acts(1)
    acts(3)
    acts(0)

    up, down = at_xy(0, 1), at_xy(0, NY - 1)
    far_up, far_down, near_up, near_down = [], [], [], []

    def far(start, size):
        at, also = pl.ds(start, size), pl.ds(HALF + start, size)
        far_up.append(send(part.at[2, at], half_in.at[0, at], up))
        far_down.append(send(part.at[2, also], half_in.at[1, at], down))

    def near_first(start, size):
        at, also = pl.ds(start, size), pl.ds(HALF + start, size)
        near_up.append(send(part.at[1, also], ig_o.at[1, also], up))
        near_down.append(send(part.at[3, at], ig_o.at[2, at], down))

    def near_last(i):
        start, size = PIECES[i]
        at, also = pl.ds(start, size), pl.ds(HALF + start, size)
        far_up[i].wait_recv()
        part[1, at] = part[1, at] + half_in[0, at]
        near_up.append(send(part.at[1, at], ig_o.at[1, at], up))
        far_down[i].wait_recv()
        part[3, also] = part[3, also] + half_in[1, at]
        near_down.append(send(part.at[3, also], ig_o.at[2, also], down))

    for copy in load_rest:
        copy.wait()

    def pick(p):
        return pl.ds(pl.multiple_of(p * FF, FF), FF)

    def factor_of(p):
        b = split_rows(basis[p])
        t = fold(mm(b, delta[pick(p), :], 1, 0))
        e = fold(mm(b, err[p], 1, 0))
        return fold(mm(split_rows(t), tok[...], 1, 0)) * SCALE + e

    partial(2)
    pl.semaphore_wait(barrier, len(greet))
    far(*PIECES[0])
    f_out[...] = factor_of(mate)
    ex_f = send(f_out, f_in, at_cx(1, 0))
    own = factor_of(c)
    ex_f.wait_recv()
    own = own + f_in[...]
    for s in range(NX * NY):
        f_src[s] = own[s * SHARE:(s + 1) * SHARE]
    rs = []
    for i, (dx, dy) in enumerate(xy):
        to = lax.rem(x + dx, NX) * NY + lax.rem(y + dy, NY)
        rs.append(send(f_src.at[to], f_rs.at[i], at_xy(dx, dy)))

    far(*PIECES[1])

    def grad_of(p):
        full[p] = mm(delta[pick(p), :], tok[...], 1, 0) * SCALE + err[p].astype(F32)

    grad_of(mate)
    ex_s = send(full.at[mate], mate_full, at_cx(1, 0))
    partial(1)

    mine = x * NY + y
    total = f_src[mine]
    for copy in rs:
        copy.wait_recv()
    for i in range(len(xy)):
        total = total + f_rs[i]
    f_z[z] = total
    fz = [send(f_z.at[z], f_z.at[z], at_z(dz)) for dz in zs]

    partial(3)
    near_first(0, 32)
    grad_of(c)
    for copy in fz:
        copy.wait_recv()
    total = f_z[0]
    for i in range(1, NZ):
        total = total + f_z[i]
    f_ag[mine] = total
    ag = [send(f_ag.at[mine], f_ag.at[mine], at_xy(dx, dy)) for dx, dy in xy]

    near_first(32, 96)

    stores = [
        pltpu.make_async_copy(full, full_o, out_sem.at[0]),
        pltpu.make_async_copy(part.at[0], ig_o.at[0], out_sem.at[1]),
        pltpu.make_async_copy(c_own, coef_o.at[c, x], out_sem.at[2]),
        pltpu.make_async_copy(stack, stack_o, out_sem.at[3]),
    ]
    stores[0].start()
    ex_s.wait_recv()
    both = (full[c] + mate_full[...]).T
    top = both.astype(BF16)
    s_high[...] = top
    s_low[...] = (both - top.astype(F32)).astype(BF16)

    for copy in ag:
        copy.wait_recv()
    for s in range(NX * NY):
        fac[s * SHARE:(s + 1) * SHARE] = f_ag[s]
    factor = fac[...]
    pair = split_rows(factor)
    coef = fold(mm(pair, s_high[...], 1, 0)) + mm(pair[:RANK], s_low[...], 1, 0)
    for j in range(NX):
        c_src[j] = coef[j * CROWS:(j + 1) * CROWS]
    crs = [
        send(c_src.at[lax.rem(x + dx, NX)], c_rs.at[x], at_cx(0, dx)) for dx in xs
    ]
    c_rs[x] = c_src[x]
    for i in range(len(PIECES)):
        near_last(i)

    sub = lax.broadcasted_iota(jnp.int32, (RANK, 2 * RANK), 0)
    lane = lax.broadcasted_iota(jnp.int32, (RANK, 2 * RANK), 1)
    gram = mm(factor, factor, 1, 1, HIGH)
    elim[:, :RANK] = gram
    elim[:, RANK:] = (sub[:, :RANK] == lane[:, :RANK]).astype(F32)

    def eliminate(k, a):
        row = jnp.sum(jnp.where(sub == k, a, 0.0), axis=0, keepdims=True)
        column = jnp.sum(jnp.where(lane == k, a, 0.0), axis=1, keepdims=True)
        pivot = jnp.sum(jnp.where(lane[:1] == k, row, 0.0), axis=1, keepdims=True)
        return a - jnp.where(sub > k, (column / pivot) * row, 0.0)

    state = lax.fori_loop(0, SPLIT, eliminate, elim[...])
    for copy in crs:
        copy.wait_recv()
    total = c_rs[0]
    for i in range(1, NX):
        total = total + c_rs[i]
    c_z[z] = total
    czs = [send(c_z.at[z], c_z.at[z], at_z(dz)) for dz in zs]

    state = lax.fori_loop(SPLIT, RANK, eliminate, state)
    left, inverse = state[:, :RANK], state[:, RANK:]
    pivots = jnp.sum(
        jnp.where(sub[:, :RANK] == lane[:, :RANK], left, 0.0), axis=1, keepdims=True
    )
    inverse = inverse * lax.rsqrt(pivots)
    hat = mm(inverse, factor, 1, 0, HIGH)
    h_own[...] = mm(inverse, hat, 0, 0, HIGH)
    ex_h = send(h_own, h_all, at_cx(1, 0))

    for copy in czs:
        copy.wait_recv()
    total = c_z[0]
    for i in range(1, NZ):
        total = total + c_z[i]
    c_own[...] = total
    cag = [send(c_own, coef_o.at[c, x], at_cx(dc, dx)) for dc, dx in cx]
    stores[2].start()

    partial(0)
    stores[1].start()
    ex_h.wait_recv()
    for p, value in ((c, h_own[...]), (mate, h_all[...])):
        top = value.astype(BF16)
        stack[p, :RANK] = top
        stack[p, RANK:2 * RANK] = top
        stack[p, 2 * RANK:] = (value - top.astype(F32)).astype(BF16)
    stores[3].start()

    for copy in near_up + near_down:
        copy.wait_recv()
    for copy in cag:
        copy.wait_recv()
    for copy in sent:
        copy.wait_send()
    for store in stores:
        store.wait()


def final_kernel(
    ig, full, coef, stack, ig_o, gu_o, uu_o, ge_o, ue_o, left, ig_v, update_v, error_v, out_sem
):
    stores = []
    for p in range(2):
        value = coef[p]
        top = value.astype(BF16)
        low = (value - top.astype(F32)).astype(BF16)
        left[p] = jnp.concatenate([top, low, top], axis=0).T
    k = 0
    for start, size in BLOCKS:
        for p, (update, error) in enumerate(((gu_o, ge_o), (uu_o, ue_o))):
            rows = pl.ds(start, size)
            approx = mm(left[p, rows], stack[p], 1, 0)
            update_v[p, rows] = approx.astype(BF16)
            error_v[p, rows] = (full[p, rows] - approx * (1.0 / (NZ * NX * NC))).astype(BF16)
            for src, dst in ((update_v, update), (error_v, error.at[0])):
                stores.append(pltpu.make_async_copy(src.at[p, rows], dst.at[rows], out_sem.at[k]))
                stores[-1].start()
                k += 1
    ig_v[...] = (ig[0] + (ig[1] + ig[2])).astype(BF16)
    stores.append(pltpu.make_async_copy(ig_v, ig_o, out_sem.at[k]))
    stores[-1].start()
    for store in stores:
        store.wait()


def on_device(tokens, hidden_grad, gate_weight, up_weight, gate_error, up_error, gate_basis, up_basis):
    V, S = pltpu.VMEM, pltpu.SemaphoreType.DMA
    any_spec = pl.BlockSpec(memory_space=pl.ANY)
    copies = 96
    ig, full, coef, stack = pl.pallas_call(
        main_kernel,
        name="main",
        out_shape=(
            V((3, ROWS, D), F32), V((2, FF, D), F32), V((2, NX, CROWS, FF), F32), V((2, 3 * RANK, D), BF16),
        ),
        in_specs=[any_spec] * 8,
        out_specs=(any_spec,) * 4,
        scratch_shapes=[
            V((TOK, D), BF16), V((FF, TOK), BF16), V((2 * FF, D), BF16),
            V((2, FF, D), BF16), V((2, RANK, FF), F32), V((2 * FF, TOK), BF16),
            V((NY, ROWS, D), F32), V((2, HALF, D), F32),
            V((2, FF, D), F32), V((FF, D), F32), V((D, FF), BF16), V((D, FF), BF16),
            V((RANK, D), F32), V((RANK, D), F32), V((NX * NY, SHARE, D), F32),
            V((NX * NY - 1, SHARE, D), F32), V((NZ, SHARE, D), F32), V((NX * NY, SHARE, D), F32),
            V((RANK, D), F32), V((RANK, 2 * RANK), F32), V((RANK, D), F32), V((RANK, D), F32),
            V((2, 3 * RANK, D), BF16),
            V((NX, CROWS, FF), F32), V((NX, CROWS, FF), F32), V((NZ, CROWS, FF), F32),
            V((CROWS, FF), F32),
            S((18,)), S((4,)), S((copies,)), S((copies,)),
        ],
        compiler_params=pltpu.CompilerParams(
            collective_id=0, has_side_effects=True, vmem_limit_bytes=40 << 20
        ),
        cost_estimate=pl.CostEstimate(
            flops=8 * TOK * D * FF, bytes_accessed=16 << 20, transcendentals=TOK * FF
        ),
    )(
        *(
            pltpu.with_memory_space_constraint(a, pltpu.HBM)
            for a in (
                tokens, hidden_grad.T, gate_weight.T, up_weight.T,
                jnp.swapaxes(gate_error, 1, 2), jnp.swapaxes(up_error, 1, 2), gate_basis, up_basis,
            )
        )
    )
    out = pltpu.HBM((FF, D), BF16)
    out_error = pltpu.HBM((1, FF, D), BF16)
    input_grad, gate_update, up_update, gate_next, up_next = pl.pallas_call(
        final_kernel,
        name="outputs",
        out_shape=(pltpu.HBM((ROWS, D), BF16), out, out, out_error, out_error),
        in_specs=[pl.BlockSpec(memory_space=V)] * 4,
        out_specs=(any_spec,) * 5,
        scratch_shapes=[
            V((2, FF, 3 * RANK), BF16), V((ROWS, D), BF16),
            V((2, FF, D), BF16), V((2, FF, D), BF16),
            S((4 * len(BLOCKS) + 1,)),
        ],
        compiler_params=pltpu.CompilerParams(vmem_limit_bytes=32 << 20),
    )(
        *(
            pltpu.with_memory_space_constraint(a, V)
            for a in (ig, full, coef.reshape(2, RANK, FF), stack)
        )
    )
    return (
        input_grad, gate_update.T, up_update.T,
        jnp.swapaxes(gate_next, 1, 2), jnp.swapaxes(up_next, 1, 2),
    )


def solution(mesh):
    placed = (
        P("dp", None),
        P("dp", "tensor"),
        P(None, "tensor"),
        P(None, "tensor"),
        P("dp", None, "tensor"),
        P("dp", None, "tensor"),
        P(None, "tensor"),
        P(None, "tensor"),
    )
    return jax.shard_map(
        on_device,
        mesh=mesh,
        in_specs=placed,
        out_specs=(
            P(("dp", "tensor"), None),
            P(None, "tensor"),
            P(None, "tensor"),
            P("dp", None, "tensor"),
            P("dp", None, "tensor"),
        ),
        check_vma=False,
    )
```

```python
import functools
import math

import jax
import jax.numpy as jnp
from jax import lax
from jax.experimental import pallas as pl
from jax.experimental.pallas import tpu as pltpu
from jax.sharding import PartitionSpec as P

MESH = pl.DeviceIdType.MESH
F32 = jnp.float32
BF16 = jnp.bfloat16
HIGH = lax.Precision.HIGHEST
NZ, NX, NC, NY = 8, 4, 2, 4
D, FF, RANK, TOK = 896, 608, 32, 1024
ROWS = TOK // NY
HALF = ROWS // 2
ORDER = (2, 1, 3, 0)
SPLIT = 10
PIECES = ((0, 32), (32, 96))
SHARE = RANK // (NX * NY)
CROWS = RANK // NX
SCALE = 1.0 / math.sqrt(TOK)
BLOCKS = ((0, 160), (160, 160), (320, 160), (480, 128))


def mm(a, b, ca, cb, precision=None):
    return lax.dot_general(
        a, b, (((ca,), (cb,)), ((), ())), precision=precision, preferred_element_type=F32
    )


def split_rows(a):
    high = a.astype(BF16)
    low = (a - high.astype(F32)).astype(BF16)
    return jnp.concatenate([high, low], axis=0)


def fold(a):
    return a[:RANK] + a[RANK:]


def device(z, x, c, y):
    return ((z * NX + x) * NC + c, y)


def main_kernel(
    tok_h, hid_h, wg_h, wu_h, eg_h, eu_h, bg_h, bu_h,
    ig_o, full_o, coef_o, stack_o,
    tok, hid, wgt, err, basis, delta, part, half_in,
    full, mate_full, s_high, s_low,
    f_out, f_in, f_src, f_rs, f_z, f_ag, fac, elim, h_own, h_all, stack,
    c_src, c_rs, c_z, c_own,
    in_sem, out_sem, send_sem, recv_sem,
):
    dp = lax.axis_index("dp")
    y = lax.axis_index("tensor")
    c = lax.rem(dp, NC)
    x = lax.rem(lax.div(dp, NC), NX)
    z = lax.div(dp, NC * NX)
    mate = 1 - c

    def chunk(k):
        return pl.ds(pl.multiple_of(lax.rem(y + k, NY) * ROWS, ROWS), ROWS)

    def local(k):
        return pl.ds(k * ROWS, ROWS)

    def load(src, dst):
        copy = pltpu.make_async_copy(src, dst, in_sem.at[len(loads)])
        copy.start()
        loads.append(copy)
        return copy

    loads = []
    load_first = [
        load(wg_h, wgt.at[pl.ds(0, FF)]), load(wu_h, wgt.at[pl.ds(FF, FF)]),
    ]
    load_chunk = {}
    for k in ORDER:
        load_chunk[k] = [
            load(tok_h.at[chunk(k)], tok.at[local(k)]),
            load(hid_h.at[:, chunk(k)], hid.at[:, local(k)]),
        ]

    def at_xy(dx, dy):
        return device(z, lax.rem(x + dx, NX), c, lax.rem(y + dy, NY))

    def at_z(dz):
        return device(lax.rem(z + dz, NZ), x, c, y)

    def at_cx(dc, dx):
        return device(z, lax.rem(x + dx, NX), lax.rem(c + dc, NC), y)

    def hops(*o):
        return -sum(min(d, n - d) for d, n in o)

    xy = [(dx, dy) for dx in range(NX) for dy in range(NY)][1:]
    xy.sort(key=lambda o: hops((o[0], NX), (o[1], NY)))
    cx = [(dc, dx) for dc in range(NC) for dx in range(NX)][1:]
    cx.sort(key=lambda o: hops((o[0], NC), (o[1], NX)))
    xs = sorted(range(1, NX), key=lambda d: hops((d, NX)))
    zs = sorted(range(1, NZ), key=lambda d: hops((d, NZ)))
    greet = [at_xy(*o) for o in xy] + [at_z(dz) for dz in range(1, NZ)]
    greet += [at_cx(*o) for o in cx if o[0] == 1]
    barrier = pltpu.get_barrier_semaphore()
    for other in greet:
        pl.semaphore_signal(barrier, inc=1, device_id=other, device_id_type=MESH)

    used = [0]
    sent = []

    def send(src, dst, to):
        i = used[0]
        used[0] += 1
        copy = pltpu.make_async_remote_copy(
            src_ref=src, dst_ref=dst, send_sem=send_sem.at[i], recv_sem=recv_sem.at[i],
            device_id=to, device_id_type=MESH,
        )
        copy.start()
        sent.append(copy)
        return copy

    def acts(k):
        cols = local(k)
        act = mm(wgt[...], tok[cols, :], 1, 1)
        g, u = act[:FF], act[FF:]
        h = hid[:, cols].astype(F32)
        s = 1.0 / (1.0 + jnp.exp(-g))
        hs = h * s
        delta[:FF, cols] = (hs * u * (1.0 + g * (1.0 - s))).astype(BF16)
        delta[FF:, cols] = (hs * g).astype(BF16)

    def partial(k):
        part[k] = mm(delta[:, local(k)], wgt[...], 0, 0)

    load_rest = [
        load(bg_h, basis.at[0]), load(bu_h, basis.at[1]),
        load(eg_h.at[0], err.at[0]), load(eu_h.at[0], err.at[1]),
    ]
    for copy in load_first:
        copy.wait()
    for k in ORDER:
        for copy in load_chunk[k]:
            copy.wait()
    acts(2)
    acts(1)
    acts(3)
    acts(0)

    up, down = at_xy(0, 1), at_xy(0, NY - 1)
    far_up, far_down, near_up, near_down = [], [], [], []

    def far(start, size):
        at, also = pl.ds(start, size), pl.ds(HALF + start, size)
        far_up.append(send(part.at[2, at], half_in.at[0, at], up))
        far_down.append(send(part.at[2, also], half_in.at[1, at], down))

    def near_first(start, size):
        at, also = pl.ds(start, size), pl.ds(HALF + start, size)
        near_up.append(send(part.at[1, also], ig_o.at[1, also], up))
        near_down.append(send(part.at[3, at], ig_o.at[2, at], down))

    def near_last(i):
        start, size = PIECES[i]
        at, also = pl.ds(start, size), pl.ds(HALF + start, size)
        far_up[i].wait_recv()
        part[1, at] = part[1, at] + half_in[0, at]
        near_up.append(send(part.at[1, at], ig_o.at[1, at], up))
        far_down[i].wait_recv()
        part[3, also] = part[3, also] + half_in[1, at]
        near_down.append(send(part.at[3, also], ig_o.at[2, also], down))

    for copy in load_rest:
        copy.wait()

    def pick(p):
        return pl.ds(pl.multiple_of(p * FF, FF), FF)

    def factor_of(p):
        b = split_rows(basis[p])
        t = fold(mm(b, delta[pick(p), :], 1, 0))
        e = fold(mm(b, err[p], 1, 0))
        return fold(mm(split_rows(t), tok[...], 1, 0)) * SCALE + e

    partial(2)
    pl.semaphore_wait(barrier, len(greet))
    far(*PIECES[0])
    f_out[...] = factor_of(mate)
    ex_f = send(f_out, f_in, at_cx(1, 0))
    own = factor_of(c)
    ex_f.wait_recv()
    own = own + f_in[...]
    for s in range(NX * NY):
        f_src[s] = own[s * SHARE:(s + 1) * SHARE]
    rs = []
    for i, (dx, dy) in enumerate(xy):
        to = lax.rem(x + dx, NX) * NY + lax.rem(y + dy, NY)
        rs.append(send(f_src.at[to], f_rs.at[i], at_xy(dx, dy)))

    far(*PIECES[1])

    def grad_of(p):
        full[p] = mm(delta[pick(p), :], tok[...], 1, 0) * SCALE + err[p].astype(F32)

    grad_of(mate)
    ex_s = send(full.at[mate], mate_full, at_cx(1, 0))
    partial(1)

    mine = x * NY + y
    total = f_src[mine]
    for copy in rs:
        copy.wait_recv()
    for i in range(len(xy)):
        total = total + f_rs[i]
    f_z[z] = total
    fz = [send(f_z.at[z], f_z.at[z], at_z(dz)) for dz in zs]

    partial(3)
    near_first(0, 32)
    grad_of(c)
    for copy in fz:
        copy.wait_recv()
    total = f_z[0]
    for i in range(1, NZ):
        total = total + f_z[i]
    f_ag[mine] = total
    ag = [send(f_ag.at[mine], f_ag.at[mine], at_xy(dx, dy)) for dx, dy in xy]

    near_first(32, 96)

    stores = [
        pltpu.make_async_copy(full, full_o, out_sem.at[0]),
        pltpu.make_async_copy(part.at[0], ig_o.at[0], out_sem.at[1]),
        pltpu.make_async_copy(c_own, coef_o.at[c, x], out_sem.at[2]),
        pltpu.make_async_copy(stack, stack_o, out_sem.at[3]),
    ]
    stores[0].start()
    ex_s.wait_recv()
    both = (full[c] + mate_full[...]).T
    top = both.astype(BF16)
    s_high[...] = top
    s_low[...] = (both - top.astype(F32)).astype(BF16)

    near_last(0)
    for copy in ag:
        copy.wait_recv()
    for s in range(NX * NY):
        fac[s * SHARE:(s + 1) * SHARE] = f_ag[s]
    factor = fac[...]
    pair = split_rows(factor)
    coef = fold(mm(pair, s_high[...], 1, 0)) + mm(pair[:RANK], s_low[...], 1, 0)
    for j in range(NX):
        c_src[j] = coef[j * CROWS:(j + 1) * CROWS]
    crs = [
        send(c_src.at[lax.rem(x + dx, NX)], c_rs.at[x], at_cx(0, dx)) for dx in xs
    ]
    c_rs[x] = c_src[x]
    near_last(1)

    sub = lax.broadcasted_iota(jnp.int32, (RANK, 2 * RANK), 0)
    lane = lax.broadcasted_iota(jnp.int32, (RANK, 2 * RANK), 1)
    gram = mm(factor, factor, 1, 1, HIGH)
    elim[:, :RANK] = gram
    elim[:, RANK:] = (sub[:, :RANK] == lane[:, :RANK]).astype(F32)

    def eliminate(k, a):
        row = jnp.sum(jnp.where(sub == k, a, 0.0), axis=0, keepdims=True)
        column = jnp.sum(jnp.where(lane == k, a, 0.0), axis=1, keepdims=True)
        pivot = jnp.sum(jnp.where(lane[:1] == k, row, 0.0), axis=1, keepdims=True)
        return a - jnp.where(sub > k, (column / pivot) * row, 0.0)

    state = lax.fori_loop(0, SPLIT, eliminate, elim[...])
    for copy in crs:
        copy.wait_recv()
    total = c_rs[0]
    for i in range(1, NX):
        total = total + c_rs[i]
    c_z[z] = total
    czs = [send(c_z.at[z], c_z.at[z], at_z(dz)) for dz in zs]

    state = lax.fori_loop(SPLIT, RANK, eliminate, state)
    left, inverse = state[:, :RANK], state[:, RANK:]
    pivots = jnp.sum(
        jnp.where(sub[:, :RANK] == lane[:, :RANK], left, 0.0), axis=1, keepdims=True
    )
    inverse = inverse * lax.rsqrt(pivots)
    hat = mm(inverse, factor, 1, 0, HIGH)
    h_own[...] = mm(inverse, hat, 0, 0, HIGH)
    ex_h = send(h_own, h_all, at_cx(1, 0))

    for copy in czs:
        copy.wait_recv()
    total = c_z[0]
    for i in range(1, NZ):
        total = total + c_z[i]
    c_own[...] = total
    cag = [send(c_own, coef_o.at[c, x], at_cx(dc, dx)) for dc, dx in cx]
    stores[2].start()

    partial(0)
    stores[1].start()
    ex_h.wait_recv()
    for p, value in ((c, h_own[...]), (mate, h_all[...])):
        top = value.astype(BF16)
        stack[p, :RANK] = top
        stack[p, RANK:2 * RANK] = top
        stack[p, 2 * RANK:] = (value - top.astype(F32)).astype(BF16)
    stores[3].start()

    for copy in near_up + near_down:
        copy.wait_recv()
    for copy in cag:
        copy.wait_recv()
    for copy in sent:
        copy.wait_send()
    for store in stores:
        store.wait()


def final_kernel(
    ig, full, coef, stack, ig_o, gu_o, uu_o, ge_o, ue_o, left, ig_v, update_v, error_v, out_sem
):
    stores = []
    for p in range(2):
        value = coef[p]
        top = value.astype(BF16)
        low = (value - top.astype(F32)).astype(BF16)
        left[p] = jnp.concatenate([top, low, top], axis=0).T
    k = 0
    for start, size in BLOCKS:
        for p, (update, error) in enumerate(((gu_o, ge_o), (uu_o, ue_o))):
            rows = pl.ds(start, size)
            approx = mm(left[p, rows], stack[p], 1, 0)
            update_v[p, rows] = approx.astype(BF16)
            error_v[p, rows] = (full[p, rows] - approx * (1.0 / (NZ * NX * NC))).astype(BF16)
            for src, dst in ((update_v, update), (error_v, error.at[0])):
                stores.append(pltpu.make_async_copy(src.at[p, rows], dst.at[rows], out_sem.at[k]))
                stores[-1].start()
                k += 1
    ig_v[...] = (ig[0] + (ig[1] + ig[2])).astype(BF16)
    stores.append(pltpu.make_async_copy(ig_v, ig_o, out_sem.at[k]))
    stores[-1].start()
    for store in stores:
        store.wait()


def on_device(tokens, hidden_grad, gate_weight, up_weight, gate_error, up_error, gate_basis, up_basis):
    V, S = pltpu.VMEM, pltpu.SemaphoreType.DMA
    any_spec = pl.BlockSpec(memory_space=pl.ANY)
    copies = 96
    ig, full, coef, stack = pl.pallas_call(
        main_kernel,
        name="main",
        out_shape=(
            V((3, ROWS, D), F32), V((2, FF, D), F32), V((2, NX, CROWS, FF), F32), V((2, 3 * RANK, D), BF16),
        ),
        in_specs=[any_spec] * 8,
        out_specs=(any_spec,) * 4,
        scratch_shapes=[
            V((TOK, D), BF16), V((FF, TOK), BF16), V((2 * FF, D), BF16),
            V((2, FF, D), BF16), V((2, RANK, FF), F32), V((2 * FF, TOK), BF16),
            V((NY, ROWS, D), F32), V((2, HALF, D), F32),
            V((2, FF, D), F32), V((FF, D), F32), V((D, FF), BF16), V((D, FF), BF16),
            V((RANK, D), F32), V((RANK, D), F32), V((NX * NY, SHARE, D), F32),
            V((NX * NY - 1, SHARE, D), F32), V((NZ, SHARE, D), F32), V((NX * NY, SHARE, D), F32),
            V((RANK, D), F32), V((RANK, 2 * RANK), F32), V((RANK, D), F32), V((RANK, D), F32),
            V((2, 3 * RANK, D), BF16),
            V((NX, CROWS, FF), F32), V((NX, CROWS, FF), F32), V((NZ, CROWS, FF), F32),
            V((CROWS, FF), F32),
            S((18,)), S((4,)), S((copies,)), S((copies,)),
        ],
        compiler_params=pltpu.CompilerParams(
            collective_id=0, has_side_effects=True, vmem_limit_bytes=40 << 20
        ),
        cost_estimate=pl.CostEstimate(
            flops=8 * TOK * D * FF, bytes_accessed=16 << 20, transcendentals=TOK * FF
        ),
    )(
        *(
            pltpu.with_memory_space_constraint(a, pltpu.HBM)
            for a in (
                tokens, hidden_grad.T, gate_weight.T, up_weight.T,
                jnp.swapaxes(gate_error, 1, 2), jnp.swapaxes(up_error, 1, 2), gate_basis, up_basis,
            )
        )
    )
    out = pltpu.HBM((FF, D), BF16)
    out_error = pltpu.HBM((1, FF, D), BF16)
    input_grad, gate_update, up_update, gate_next, up_next = pl.pallas_call(
        final_kernel,
        name="outputs",
        out_shape=(pltpu.HBM((ROWS, D), BF16), out, out, out_error, out_error),
        in_specs=[pl.BlockSpec(memory_space=V)] * 4,
        out_specs=(any_spec,) * 5,
        scratch_shapes=[
            V((2, FF, 3 * RANK), BF16), V((ROWS, D), BF16),
            V((2, FF, D), BF16), V((2, FF, D), BF16),
            S((4 * len(BLOCKS) + 1,)),
        ],
        compiler_params=pltpu.CompilerParams(vmem_limit_bytes=32 << 20),
    )(
        *(
            pltpu.with_memory_space_constraint(a, V)
            for a in (ig, full, coef.reshape(2, RANK, FF), stack)
        )
    )
    return (
        input_grad, gate_update.T, up_update.T,
        jnp.swapaxes(gate_next, 1, 2), jnp.swapaxes(up_next, 1, 2),
    )


def solution(mesh):
    placed = (
        P("dp", None),
        P("dp", "tensor"),
        P(None, "tensor"),
        P(None, "tensor"),
        P("dp", None, "tensor"),
        P("dp", None, "tensor"),
        P(None, "tensor"),
        P(None, "tensor"),
    )
    return jax.shard_map(
        on_device,
        mesh=mesh,
        in_specs=placed,
        out_specs=(
            P(("dp", "tensor"), None),
            P(None, "tensor"),
            P(None, "tensor"),
            P("dp", None, "tensor"),
            P("dp", None, "tensor"),
        ),
        check_vma=False,
    )
```
